512 devices in a mesh: cells: 16 (over y, z_lo), row: 4 (over z_hi), col: 8 (over x, core).
Axes of the slice: x: 4, y: 4, z: 16 (z_hi: 4, z_lo: 4; z = z_hi * 4 + z_lo), core: 2. Of those that a mesh axis runs over, the one named last changes fastest.
Arguments:
- snapshots: bfloat16 [2048, 131072], P('row', ('cells', 'col')), may hold values from -8 to 8
- snapshot_order: int32 [2048], replicated, may hold values from 0 to 2047, each once
Outputs:
- gram: float32 [2048, 2048], P('row', ('cells', 'col'))
The draws below stay inside these ranges and needn't reach their ends.
All inputs are finite; a program needn't handle non-finite values.
Results may differ from the reference program's by a relative error of at most 0.0003.
Values may be sent and summed in bfloat16 or wider, within the bound.
No kernel may reach another device: no remote copies, remote signals or barrier semaphores. Data moves between devices by JAX's collectives and lax.ppermute only.
A program may use at most 64 MiB of HBM per device.

```python
import jax
import jax.numpy as jnp
from jax import lax

M = 2048
CELLS = 131072


def draw_snapshots(key, part):
    key = jax.random.fold_in(key, 11)
    key_place, key_freq, key_phase, key_jitter, key_amp = jax.random.split(key, 5)
    places = jax.random.uniform(key_place, (M, 3), jnp.float32, 0.0, 4.0)
    frequency = jnp.clip(jax.random.cauchy(key_freq, (3, CELLS), jnp.float32), -40.0, 40.0)
    phases = jax.random.uniform(key_phase, (1, CELLS), jnp.float32, -3.14159265, 3.14159265)
    angles = places[:, 0:1] * frequency[0:1, :] + places[:, 1:2] * frequency[1:2, :]
    angles = angles + places[:, 2:3] * frequency[2:3, :] + phases
    wavefield = 1.27 * jnp.cos(angles)
    jitter = 0.45 * jax.random.normal(key_jitter, (M, CELLS), jnp.float32)
    amplitude = jax.random.uniform(key_amp, (M, 1), jnp.float32, 0.6, 1.4)
    values = (wavefield + jitter) * amplitude
    return jnp.clip(values, -8.0, 8.0).astype(jnp.bfloat16)


def setup_inputs(seed: int = 0) -> dict:
    key_of = jax.random.split(jax.random.key(seed), 3)
    snapshots = draw_snapshots(jax.random.fold_in(key_of[2], 71), 0)
    snapshot_order = jax.random.permutation(key_of[1], M).astype(jnp.int32)
    return dict(snapshots=snapshots, snapshot_order=snapshot_order)


def reference(snapshots, snapshot_order):
    ordered = jnp.take(snapshots, snapshot_order.astype(jnp.int32), axis=0).astype(jnp.float32)
    gram = jnp.dot(ordered, ordered.T, precision=lax.Precision.HIGHEST, preferred_element_type=jnp.float32)
    return gram * (1.0 / CELLS)
```

```python
import jax
import jax.numpy as jnp
from jax import lax
from jax.sharding import Mesh, PartitionSpec as P


def shift(value, axis, by):
    n = lax.axis_size(axis)
    return lax.ppermute(value, axis, [(i, (i + by) % n) for i in range(n)])


def local(snapshots, snapshot_order):
    held, cells = snapshots.shape
    rows = lax.axis_size("row")
    total = held * rows
    devices = lax.axis_size(("y", "zl", "row", "x", "core"))
    factor = 1.0 / (cells * (devices // rows))
    part = cells // rows
    split = snapshots.reshape(held, rows, part).transpose(1, 0, 2)
    mine = lax.all_to_all(split, "row", 0, 0, tiled=False).reshape(total, part)
    pick = (snapshot_order[:, None] == lax.iota(jnp.int32, total)[None, :]).astype(jnp.bfloat16)
    mine = jnp.dot(pick, mine, preferred_element_type=jnp.float32).astype(jnp.bfloat16)
    own = [mine] + [shift(mine, "x", by) for by in (1, 3, 2)]
    pieces = own + [shift(p, "core", 1) for p in own]
    everything = jnp.concatenate(pieces, axis=1)
    sub = lax.axis_size("x") * lax.axis_size("core")
    width = total // (lax.axis_size(("y", "zl", "x", "core")))
    at = lax.axis_index(("x", "core"))
    chosen = everything.reshape(total // (sub * width), sub, width, everything.shape[1])
    chosen = lax.dynamic_index_in_dim(chosen, at, 1, keepdims=False).reshape(total // sub, -1)
    value = lax.dot_general(
        chosen, everything, (((1,), (1,)), ((), ())), preferred_element_type=jnp.float32
    )
    for axis in ("y", "zl"):
        n = lax.axis_size(axis)
        value = value.reshape(n, value.shape[0] // n, total)
        value = lax.all_to_all(value, axis, 0, 0, tiled=False).sum(0)
    value = value.reshape(width, rows, held).transpose(1, 0, 2)
    value = lax.all_to_all(value, "row", 0, 0, tiled=False).sum(0)
    return value.T * factor


def solution(mesh):
    fine = Mesh(mesh.devices.reshape(4, 4, 4, 4, 2), ("y", "zl", "row", "x", "core"))
    columns = ("y", "zl", "x", "core")
    return jax.shard_map(
        local, mesh=fine, in_specs=(P("row", columns), P()), out_specs=P("row", columns), check_vma=False
    )
```

```python
import functools

import jax
import jax.numpy as jnp
from jax import lax
from jax.experimental import pallas as pl
from jax.experimental.pallas import tpu as pltpu
from jax.sharding import Mesh, PartitionSpec as P

Y, ZL, ROW, X, CORE = 4, 4, 4, 4, 2
CHUNKS = 2
VMEM_BYTES = 40 * 1024 * 1024
STEPS = (1, 3, 2)


def shift(value, axis, by):
    n = lax.axis_size(axis)
    return lax.ppermute(value, axis, [(i, (i + by) % n) for i in range(n)])


def params():
    return pltpu.CompilerParams(vmem_limit_bytes=VMEM_BYTES)


def split_kernel(place, source, *outs):
    row = place[0]
    width = outs[0].shape[1]
    for chunk in range(CHUNKS):
        for k in range(ROW):
            start = lax.rem(row + k, ROW) * (width * CHUNKS) + chunk * width
            outs[chunk * ROW + k][...] = source[:, pl.ds(pl.multiple_of(start, width), width)]


def split(place, snapshots):
    held, cells = snapshots.shape
    width = cells // (ROW * CHUNKS)
    return pl.pallas_call(
        split_kernel,
        out_shape=[jax.ShapeDtypeStruct((held, width), snapshots.dtype)] * (CHUNKS * ROW),
        in_specs=[pl.BlockSpec(memory_space=pltpu.SMEM), pl.BlockSpec(memory_space=pltpu.VMEM)],
        out_specs=[pl.BlockSpec(memory_space=pltpu.VMEM)] * (CHUNKS * ROW),
        compiler_params=params(),
        name="split_cells",
    )(place, snapshots)


def order_kernel(index, *refs):
    pieces, out = refs[:-1], refs[-1]
    block = 256
    held = pieces[0].shape[0]
    for at in range(0, out.shape[0], block):
        wanted = index[at : at + block, :]
        value = None
        for k, piece in enumerate(pieces):
            row = lax.broadcasted_iota(jnp.int32, (block, held), 1) + k * held
            pick = jnp.where(wanted == row, 1.0, 0.0).astype(jnp.bfloat16)
            term = jnp.dot(pick, piece[...], preferred_element_type=jnp.float32)
            value = term if value is None else value + term
        out[at : at + block, :] = value.astype(out.dtype)


def in_order(index, pieces):
    total = index.shape[0]
    width = pieces[0].shape[1]
    return pl.pallas_call(
        order_kernel,
        out_shape=jax.ShapeDtypeStruct((total, width), pieces[0].dtype),
        in_specs=[pl.BlockSpec(memory_space=pltpu.VMEM)] * (1 + len(pieces)),
        out_specs=pl.BlockSpec(memory_space=pltpu.VMEM),
        compiler_params=params(),
        cost_estimate=pl.CostEstimate(
            flops=2 * total * total * width, bytes_accessed=4 * total * width, transcendentals=0
        ),
        name="rows_in_order",
    )(index, *pieces)


D_ORDER = (2, 1, 3, 0)


def panel_kernel(count, place, *refs):
    pieces, outs, chosen = refs[:count], refs[count:-1], refs[-1]
    y, zl, row, x, core = (place[i] for i in (1, 2, 0, 3, 4))
    width = pieces[0].shape[1]
    total = pieces[0].shape[0]
    unit = total // (Y * ZL * X * CORE)
    step = pl.program_id(0)

    @pl.when(step == 0)
    def _():
        for part in range(CORE):
            to_core = lax.rem(core + 1 - part, CORE)
            for d_at, d in enumerate(D_ORDER):
                for k in range(ZL):
                    to_y, to_zl = lax.rem(y + d, Y), lax.rem(zl + k, ZL)
                    start = (((to_y * ZL + to_zl) * X + x) * CORE + to_core) * unit
                    at = ((part * Y + d_at) * ZL + k) * unit
                    for p, piece in enumerate(pieces):
                        chosen[at : at + unit, p * width : (p + 1) * width] = piece[
                            pl.ds(pl.multiple_of(start, unit), unit), :
                        ]

    columns = outs[0].shape[1]
    per_row = total // ROW // columns
    start = lax.rem(row + step // per_row, ROW) * (total // ROW) + lax.rem(step, per_row) * columns
    rows = pl.ds(pl.multiple_of(start, columns), columns)
    right = jnp.concatenate([piece[rows, :] for piece in pieces], axis=1)
    value = lax.dot_general(
        chosen[...], right, (((1,), (1,)), ((), ())), preferred_element_type=jnp.float32
    )
    at = 0
    for out in outs:
        out[...] = value[at : at + out.shape[0], :]
        at += out.shape[0]


def panel(place, pieces):
    total, width = pieces[0].shape
    columns = 256
    height = total // (Y * X * CORE)
    heights = [height, 2 * height, height] * CORE
    depth = width * len(pieces)
    return pl.pallas_call(
        functools.partial(panel_kernel, len(pieces)),
        grid=(total // columns,),
        out_shape=[jax.ShapeDtypeStruct((h, total), jnp.float32) for h in heights],
        in_specs=[pl.BlockSpec(memory_space=pltpu.SMEM)]
        + [pl.BlockSpec(memory_space=pltpu.VMEM)] * len(pieces),
        out_specs=[pl.BlockSpec((h, columns), lambda i: (0, i)) for h in heights],
        scratch_shapes=[pltpu.VMEM((total // X, depth), pieces[0].dtype)],
        compiler_params=params(),
        cost_estimate=pl.CostEstimate(
            flops=2 * total * (total // X) * depth,
            bytes_accessed=2 * total * depth + 4 * total * (total // X),
            transcendentals=0,
        ),
        name="gram_panel",
    )(place, *pieces)


def local(snapshots, snapshot_order):
    held, cells = snapshots.shape
    total = held * ROW
    factor = 1.0 / (cells * Y * ZL * X * CORE)
    row = lax.axis_index("row")
    place = jnp.stack([row] + [lax.axis_index(a) for a in ("y", "zl", "x", "core")])
    index = lax.rem(row - snapshot_order // held + ROW, ROW) * held + snapshot_order % held
    index = index.reshape(total, 1)
    parts = split(place, snapshots)
    pieces = []
    for chunk in range(CHUNKS):
        sent = parts[chunk * ROW : (chunk + 1) * ROW]
        got = {k: shift(sent[k], "row", k) for k in STEPS}
        mine = in_order(index, [sent[0]] + [got[k] for k in (1, 2, 3)])
        pieces += [mine] + [shift(mine, "x", by) for by in STEPS]
    far, near, own, keep_far, keep_near, keep_own = panel(place, pieces)
    height = far.shape[0]
    far = keep_far + shift(far, "core", 1)
    near = keep_near + shift(near, "core", 1)
    own = keep_own + shift(own, "core", 1)
    value = (
        own
        + shift(near[:height], "y", 1)
        + shift(near[height:], "y", 3)
        + shift(far, "y", 2)
    )
    unit = height // ZL
    value = value[:unit] + sum(shift(value[k * unit : (k + 1) * unit], "zl", k) for k in STEPS)
    value = value[:, :held] + sum(
        shift(value[:, k * held : (k + 1) * held], "row", k) for k in STEPS
    )
    return value.T * factor


def solution(mesh):
    fine = Mesh(mesh.devices.reshape(Y, ZL, ROW, X, CORE), ("y", "zl", "row", "x", "core"))
    columns = ("y", "zl", "x", "core")
    return jax.shard_map(
        local, mesh=fine, in_specs=(P("row", columns), P()), out_specs=P("row", columns), check_vma=False
    )
```

```python
import jax
import jax.numpy as jnp
from jax import lax
from jax.experimental import pallas as pl
from jax.experimental.pallas import tpu as pltpu
from jax.sharding import Mesh, PartitionSpec as P

Y, ZL, ROW, X, CORE = 4, 4, 4, 4, 2
VMEM_BYTES = 40 * 1024 * 1024
FULL = pl.BlockSpec(memory_space=pltpu.VMEM)
SCALARS = pl.BlockSpec(memory_space=pltpu.SMEM)


def params():
    return pltpu.CompilerParams(vmem_limit_bytes=VMEM_BYTES)


def both_ways(value, axis, by):
    n = lax.axis_size(axis)
    pairs = [(i * CORE + c, (i + (by if c == 0 else -by)) % n * CORE + c) for i in range(n) for c in range(CORE)]
    return lax.ppermute(value, (axis, "core"), pairs)


def split_kernel(place, source, *outs):
    row, core = place[0], place[1]
    width = outs[0].shape[1]
    for out, step in zip(outs, (0, 1 + 2 * core, 3 + 2 * core, 2)):
        start = lax.rem(row + step, ROW) * width
        out[...] = source[:, pl.ds(pl.multiple_of(start, width), width)]


STEPS = (1, 3, 2)


def split(place, snapshots):
    held, cells = snapshots.shape
    width = cells // ROW
    return pl.pallas_call(
        split_kernel,
        out_shape=[jax.ShapeDtypeStruct((held, width), snapshots.dtype)] * ROW,
        in_specs=[SCALARS, FULL],
        out_specs=[FULL] * ROW,
        compiler_params=params(),
        name="split_cells",
    )(place, snapshots)


def panel_kernel(place, wanted, *refs):
    pieces, (far, near, rows, chosen) = refs[:ROW], refs[ROW:]
    _, held, width = pieces[0].shape
    total, depth = rows.shape
    step = pl.program_id(0)

    @pl.when(step == 0)
    def _():
        row, core = place[0], place[1]
        for m, back in enumerate((0, 3 + 2 * core, 1 + 2 * core, 2)):
            at = pl.ds(pl.multiple_of(lax.rem(row + back, ROW) * held, held), held)
            for s in range(X):
                rows[at, s * width : (s + 1) * width] = pieces[m][s]
        block = 256
        for at in range(0, wanted.shape[0], block):
            number = lax.broadcasted_iota(jnp.int32, (block, total), 1)
            pick = jnp.where(wanted[at : at + block, :] == number, 1.0, 0.0).astype(jnp.bfloat16)
            for s in range(0, depth, width):
                chosen[at : at + block, s : s + width] = jnp.dot(
                    pick, rows[:, s : s + width], preferred_element_type=jnp.float32
                ).astype(jnp.bfloat16)

    lanes = far.shape[1]
    right = rows[pl.ds(pl.multiple_of(step * lanes, lanes), lanes), :]
    half = far.shape[0]
    for part, out in enumerate((far, near)):
        out[...] = lax.dot_general(
            chosen[part * half : (part + 1) * half, :],
            right,
            (((1,), (1,)), ((), ())),
            preferred_element_type=jnp.float32,
        )


def panel(place, wanted, pieces):
    _, held, width = pieces[0].shape
    total, depth, lanes = held * ROW, width * X, 512
    count = wanted.shape[0]
    half = count // CORE
    return pl.pallas_call(
        panel_kernel,
        grid=(total // lanes,),
        out_shape=[jax.ShapeDtypeStruct((half, total), jnp.float32)] * CORE,
        in_specs=[SCALARS] + [FULL] * (1 + len(pieces)),
        out_specs=[pl.BlockSpec((half, lanes), lambda i: (0, i))] * CORE,
        scratch_shapes=[
            pltpu.VMEM((total, depth), jnp.bfloat16),
            pltpu.VMEM((count, depth), jnp.bfloat16),
        ],
        compiler_params=params(),
        cost_estimate=pl.CostEstimate(
            flops=4 * count * total * depth,
            bytes_accessed=2 * total * depth + 4 * count * total,
            transcendentals=0,
        ),
        name="gram_panel",
    )(place, wanted, *pieces)


def arrange_kernel(order, value, out):
    whole = (value[0] + value[1]) + (value[2] + value[3])
    high = whole.astype(jnp.bfloat16)
    rest = whole - high.astype(jnp.float32)
    middle = rest.astype(jnp.bfloat16)
    low = (rest - middle.astype(jnp.float32)).astype(jnp.bfloat16)
    parts = jnp.concatenate([high, middle, low], axis=0)
    count, total = whole.shape
    _, unit, held = out.shape
    block = 256
    for at in range(0, total, block):
        number = lax.broadcasted_iota(jnp.int32, (total, block), 0)
        pick = jnp.where(order[:, at : at + block] == number, 1.0, 0.0).astype(jnp.bfloat16)
        moved = jnp.dot(parts, pick, preferred_element_type=jnp.float32)
        moved = (moved[:count] + moved[count : 2 * count]) + moved[2 * count :]
        row, lane = at // held, at % held
        for zl in range(ZL):
            out[row * ZL + zl, :, lane : lane + block] = moved[zl * unit : (zl + 1) * unit]


def arrange(order, value):
    _, count, total = value.shape
    return pl.pallas_call(
        arrange_kernel,
        out_shape=jax.ShapeDtypeStruct((ROW * ZL, count // ZL, total // ROW), jnp.float32),
        in_specs=[FULL, FULL],
        out_specs=FULL,
        compiler_params=params(),
        cost_estimate=pl.CostEstimate(
            flops=6 * count * total * total, bytes_accessed=20 * count * total, transcendentals=0
        ),
        name="arrange_rows",
    )(order, value)


def local(snapshots, snapshot_order):
    held, cells = snapshots.shape
    total = held * ROW
    factor = 1.0 / (cells * Y * ZL * X * CORE)
    core = lax.axis_index("core")
    place = jnp.stack([lax.axis_index("row"), core])
    order = snapshot_order.reshape(1, total)
    mine = snapshot_order.reshape(Y, ZL, X, CORE, -1)
    mine = lax.dynamic_index_in_dim(mine, lax.axis_index("x"), 2, keepdims=False)
    mine = mine.transpose(2, 0, 1, 3)
    wanted = jnp.where(core == 0, mine[::-1], mine).reshape(total // X, 1)
    own, *sent = split(place, snapshots)
    got = [both_ways(value, "row", by) for value, by in zip(sent, STEPS)]
    pieces = [lax.all_gather(own, "x")]
    for value in got:
        if len(pieces) > 1:
            value, _ = lax.optimization_barrier((value, pieces[-1]))
        copies = jnp.broadcast_to(value[None], (X,) + value.shape)
        pieces.append(lax.all_to_all(copies, "x", 0, 0, tiled=False))
    far, near = panel(place, wanted, pieces)
    near = near + lax.ppermute(far, "core", [(0, 1), (1, 0)])
    value = lax.all_to_all(near.reshape(Y, -1, total), "y", 0, 0, tiled=False)
    value = arrange(order, value)
    value = lax.all_to_all(value, ("row", "zl"), 0, 0, tiled=False)
    return value.sum(0).T * factor


def solution(mesh):
    fine = Mesh(mesh.devices.reshape(Y, ZL, ROW, X, CORE), ("y", "zl", "row", "x", "core"))
    columns = ("y", "zl", "x", "core")
    return jax.shard_map(
        local, mesh=fine, in_specs=(P("row", columns), P()), out_specs=P("row", columns), check_vma=False
    )
```

```python
import jax
import jax.numpy as jnp
from jax import lax
from jax.experimental import pallas as pl
from jax.experimental.pallas import tpu as pltpu
from jax.sharding import Mesh, PartitionSpec as P

Y, ZL, ROW, X, CORE = 4, 4, 4, 4, 2
VMEM_BYTES = 40 * 1024 * 1024
FULL = pl.BlockSpec(memory_space=pltpu.VMEM)
SCALARS = pl.BlockSpec(memory_space=pltpu.SMEM)


def params():
    return pltpu.CompilerParams(vmem_limit_bytes=VMEM_BYTES)


def both_ways(value, axis, by):
    n = lax.axis_size(axis)
    pairs = [(i * CORE + c, (i + (by if c == 0 else -by)) % n * CORE + c) for i in range(n) for c in range(CORE)]
    return lax.ppermute(value, (axis, "core"), pairs)


def split_kernel(place, source, *outs):
    row, core = place[0], place[1]
    width = outs[0].shape[1]
    for out, step in zip(outs, (0, 1 + 2 * core, 3 + 2 * core, 2)):
        start = lax.rem(row + step, ROW) * width
        out[...] = source[:, pl.ds(pl.multiple_of(start, width), width)]


STEPS = (1, 3, 2)


def split(place, snapshots):
    held, cells = snapshots.shape
    width = cells // ROW
    return pl.pallas_call(
        split_kernel,
        out_shape=[jax.ShapeDtypeStruct((held, width), snapshots.dtype)] * ROW,
        in_specs=[SCALARS, FULL],
        out_specs=[FULL] * ROW,
        compiler_params=params(),
        name="split_cells",
    )(place, snapshots)


def slots(place):
    x, core = place[2], place[1]
    return [lax.rem(x + back, X) for back in (0, 3 + 2 * core, 1 + 2 * core, 2)]


def rows_of(m, at, count, order, own, opposite, pairs):
    if m in (0, 3):
        ref = own if m == 0 else opposite
        return [ref[slot, at : at + count, :] for slot in order]
    at += (m - 1) * own.shape[1]
    return [ref[at : at + count, :] for ref in pairs]


BLOCK = 256


def multiply(left, out, blocks, order, own, opposite, pairs):
    held = own.shape[1]
    for to, m in enumerate(blocks):
        for at in range(0, held, BLOCK):
            right = jnp.concatenate(rows_of(m, at, BLOCK, order, own, opposite, pairs), axis=1)
            out[:, to * held + at : to * held + at + BLOCK] = lax.dot_general(
                left, right, (((1,), (1,)), ((), ())), preferred_element_type=jnp.float32
            )


def far_kernel(place, wanted, own, opposite, p0, p1, p2, p3, far, chosen):
    pairs = (p0, p1, p2, p3)
    order = slots(place)
    held = own.shape[1]
    values = []
    for at in range(0, wanted.shape[0], BLOCK):
        parts = [None] * X
        for m in range(ROW):
            number = lax.broadcasted_iota(jnp.int32, (BLOCK, held), 1) + m * held
            pick = jnp.where(wanted[at : at + BLOCK, :] == number, 1.0, 0.0).astype(jnp.bfloat16)
            for s, rows in enumerate(rows_of(m, 0, held, order, own, opposite, pairs)):
                term = jnp.dot(pick, rows, preferred_element_type=jnp.float32)
                parts[s] = term if parts[s] is None else parts[s] + term
        values.append(jnp.concatenate(parts, axis=1).astype(jnp.bfloat16))
    chosen[...] = values[1]
    multiply(values[0], far, (0, 2, 1, 3), order, own, opposite, pairs)


def near_kernel(place, chosen, own, opposite, p0, p1, p2, p3, near):
    multiply(chosen[...], near, (0, 1, 2, 3), slots(place), own, opposite, (p0, p1, p2, p3))


def panels(place, wanted, own, opposite, pairs):
    _, held, width = own.shape
    total, depth, half = held * ROW, width * X, wanted.shape[0] // CORE
    panel = jax.ShapeDtypeStruct((half, total), jnp.float32)
    cost = pl.CostEstimate(
        flops=2 * half * total * depth, bytes_accessed=2 * total * depth + 4 * half * total, transcendentals=0
    )
    far, chosen = pl.pallas_call(
        far_kernel,
        out_shape=[panel, jax.ShapeDtypeStruct((half, depth), own.dtype)],
        in_specs=[SCALARS] + [FULL] * (3 + X),
        out_specs=[FULL] * 2,
        compiler_params=params(),
        cost_estimate=cost,
        name="far_panel",
    )(place, wanted, own, opposite, *pairs)
    near = pl.pallas_call(
        near_kernel,
        out_shape=panel,
        in_specs=[SCALARS] + [FULL] * (3 + X),
        out_specs=FULL,
        compiler_params=params(),
        cost_estimate=cost,
        name="near_panel",
    )(place, chosen, own, opposite, *pairs)
    return far, near


def arrange_kernel(order, value, out):
    whole = (value[0] + value[1]) + (value[2] + value[3])
    high = whole.astype(jnp.bfloat16)
    rest = whole - high.astype(jnp.float32)
    middle = rest.astype(jnp.bfloat16)
    low = (rest - middle.astype(jnp.float32)).astype(jnp.bfloat16)
    parts = jnp.concatenate([high, middle, low], axis=0)
    count, total = whole.shape
    _, unit, held = out.shape
    block = 256
    for at in range(0, total, block):
        number = lax.broadcasted_iota(jnp.int32, (total, block), 0)
        pick = jnp.where(order[:, at : at + block] == number, 1.0, 0.0).astype(jnp.bfloat16)
        moved = jnp.dot(parts, pick, preferred_element_type=jnp.float32)
        moved = (moved[:count] + moved[count : 2 * count]) + moved[2 * count :]
        row, lane = at // held, at % held
        for zl in range(ZL):
            out[row * ZL + zl, :, lane : lane + block] = moved[zl * unit : (zl + 1) * unit]


def arrange(order, value):
    _, count, total = value.shape
    return pl.pallas_call(
        arrange_kernel,
        out_shape=jax.ShapeDtypeStruct((ROW * ZL, count // ZL, total // ROW), jnp.float32),
        in_specs=[FULL, FULL],
        out_specs=FULL,
        compiler_params=params(),
        cost_estimate=pl.CostEstimate(
            flops=6 * count * total * total, bytes_accessed=20 * count * total, transcendentals=0
        ),
        name="arrange_rows",
    )(order, value)


def share(value):
    copies = jnp.broadcast_to(value[None], (X,) + value.shape)
    return lax.all_to_all(copies, "x", 0, 0, tiled=False)


def local(snapshots, snapshot_order):
    held, cells = snapshots.shape
    total = held * ROW
    factor = 1.0 / (cells * Y * ZL * X * CORE)
    core = lax.axis_index("core")
    row = lax.axis_index("row")
    place = jnp.stack([row, core, lax.axis_index("x")])
    away = lax.rem(snapshot_order // held - row + ROW, ROW)
    first = jnp.where(core == 0, ROW - 1, 1)
    piece = jnp.where(away == 0, 0, jnp.where(away == 2, 3, jnp.where(away == first, 1, 2)))
    index = piece * held + snapshot_order % held
    mine = index.reshape(Y, ZL, X, CORE, -1)
    mine = lax.dynamic_index_in_dim(mine, lax.axis_index("x"), 2, keepdims=False)
    mine = mine.transpose(2, 0, 1, 3)
    wanted = jnp.where(core == 0, mine[::-1], mine).reshape(total // X, 1)
    own, *sent = split(place, snapshots)
    near_a, near_b, opposite = [both_ways(value, "row", by) for value, by in zip(sent, STEPS)]
    own = lax.all_gather(own, "x")
    pair = jnp.concatenate([near_a, near_b], axis=0)
    pairs = [pair] + [both_ways(pair, "x", by) for by in STEPS]
    opposite = share(opposite)
    far, near = panels(place, wanted, own, opposite, pairs)
    near = near + lax.ppermute(far, "core", [(0, 1), (1, 0)])
    value = lax.all_to_all(near.reshape(Y, -1, total), "y", 0, 0, tiled=False)
    value = arrange(index.reshape(1, total), value)
    value = lax.all_to_all(value, ("row", "zl"), 0, 0, tiled=False)
    return value.sum(0).T * factor


def solution(mesh):
    fine = Mesh(mesh.devices.reshape(Y, ZL, ROW, X, CORE), ("y", "zl", "row", "x", "core"))
    columns = ("y", "zl", "x", "core")
    return jax.shard_map(
        local, mesh=fine, in_specs=(P("row", columns), P()), out_specs=P("row", columns), check_vma=False
    )
```

```python
import functools

import jax
import jax.numpy as jnp
from jax import lax
from jax.experimental import pallas as pl
from jax.experimental.pallas import tpu as pltpu
from jax.sharding import Mesh, PartitionSpec as P

Y, ZL, ROW, X, CORE = 4, 4, 4, 4, 2
VMEM_BYTES = 40 * 1024 * 1024
FULL = pl.BlockSpec(memory_space=pltpu.VMEM)
SCALARS = pl.BlockSpec(memory_space=pltpu.SMEM)


def params():
    return pltpu.CompilerParams(vmem_limit_bytes=VMEM_BYTES)


def both_ways(value, axis, by):
    n = lax.axis_size(axis)
    pairs = [(i * CORE + c, (i + (by if c == 0 else -by)) % n * CORE + c) for i in range(n) for c in range(CORE)]
    return lax.ppermute(value, (axis, "core"), pairs)


def split_kernel(place, source, *outs):
    row, core = place[0], place[1]
    width = outs[0].shape[1]
    for out, step in zip(outs, (0, 1 + 2 * core, 3 + 2 * core, 2)):
        start = lax.rem(row + step, ROW) * width
        out[...] = source[:, pl.ds(pl.multiple_of(start, width), width)]


STEPS = (1, 3, 2)


def split(place, snapshots):
    held, cells = snapshots.shape
    width = cells // ROW
    return pl.pallas_call(
        split_kernel,
        out_shape=[jax.ShapeDtypeStruct((held, width), snapshots.dtype)] * ROW,
        in_specs=[SCALARS, FULL],
        out_specs=[FULL] * ROW,
        compiler_params=params(),
        name="split_cells",
    )(place, snapshots)


def slots(place):
    x, core = place[2], place[1]
    return [lax.rem(x + back, X) for back in (0, 3 + 2 * core, 1 + 2 * core, 2)]


def rows_of(source, at, count, order, arrays):
    kind, which, start = source
    at += start
    if kind == "by_x":
        return [arrays[which][slot, at : at + count, :] for slot in order]
    if kind == "stack":
        return [arrays[which][s, at : at + count, :] for s in range(X)]
    return [arrays[i][at : at + count, :] for i in which]


BLOCK = 256


def multiply(left, out, sources, held, order, arrays):
    for to, source in enumerate(sources):
        for at in range(0, held, BLOCK):
            right = jnp.concatenate(rows_of(source, at, BLOCK, order, arrays), axis=1)
            out[:, to * held + at : to * held + at + BLOCK] = lax.dot_general(
                left, right, (((1,), (1,)), ((), ())), preferred_element_type=jnp.float32
            )


def far_kernel(sources, held, place, wanted, *refs):
    arrays, (far, chosen) = refs[:-2], refs[-2:]
    order = slots(place)
    values = []
    for at in range(0, wanted.shape[0], BLOCK):
        parts = [None] * X
        for m, source in enumerate(sources):
            number = lax.broadcasted_iota(jnp.int32, (BLOCK, held), 1) + m * held
            pick = jnp.where(wanted[at : at + BLOCK, :] == number, 1.0, 0.0).astype(jnp.bfloat16)
            for s, rows in enumerate(rows_of(source, 0, held, order, arrays)):
                term = jnp.dot(pick, rows, preferred_element_type=jnp.float32)
                parts[s] = term if parts[s] is None else parts[s] + term
        values.append(jnp.concatenate(parts, axis=1).astype(jnp.bfloat16))
    chosen[...] = values[1]
    multiply(values[0], far, [sources[m] for m in (0, 2, 1, 3)], held, order, arrays)


def near_kernel(sources, held, place, chosen, *refs):
    arrays, near = refs[:-1], refs[-1]
    multiply(chosen[...], near, sources, held, slots(place), arrays)


def panels(place, wanted, held, sources, arrays):
    width = arrays[0].shape[-1]
    total, depth, half = held * ROW, width * X, wanted.shape[0] // CORE
    panel = jax.ShapeDtypeStruct((half, total), jnp.float32)
    cost = pl.CostEstimate(
        flops=2 * half * total * depth, bytes_accessed=2 * total * depth + 4 * half * total, transcendentals=0
    )
    far, chosen = pl.pallas_call(
        functools.partial(far_kernel, sources, held),
        out_shape=[panel, jax.ShapeDtypeStruct((half, depth), arrays[0].dtype)],
        in_specs=[SCALARS] + [FULL] * (1 + len(arrays)),
        out_specs=[FULL] * 2,
        compiler_params=params(),
        cost_estimate=cost,
        name="far_panel",
    )(place, wanted, *arrays)
    near = pl.pallas_call(
        functools.partial(near_kernel, sources, held),
        out_shape=panel,
        in_specs=[SCALARS] + [FULL] * (1 + len(arrays)),
        out_specs=FULL,
        compiler_params=params(),
        cost_estimate=cost,
        name="near_panel",
    )(place, chosen, *arrays)
    return far, near


def arrange_kernel(order, value, out):
    whole = (value[0] + value[1]) + (value[2] + value[3])
    high = whole.astype(jnp.bfloat16)
    rest = whole - high.astype(jnp.float32)
    middle = rest.astype(jnp.bfloat16)
    low = (rest - middle.astype(jnp.float32)).astype(jnp.bfloat16)
    parts = jnp.concatenate([high, middle, low], axis=0)
    count, total = whole.shape
    _, unit, held = out.shape
    block = 256
    for at in range(0, total, block):
        number = lax.broadcasted_iota(jnp.int32, (total, block), 0)
        pick = jnp.where(order[:, at : at + block] == number, 1.0, 0.0).astype(jnp.bfloat16)
        moved = jnp.dot(parts, pick, preferred_element_type=jnp.float32)
        moved = (moved[:count] + moved[count : 2 * count]) + moved[2 * count :]
        row, lane = at // held, at % held
        for zl in range(ZL):
            out[row * ZL + zl, :, lane : lane + block] = moved[zl * unit : (zl + 1) * unit]


def arrange(order, value):
    _, count, total = value.shape
    return pl.pallas_call(
        arrange_kernel,
        out_shape=jax.ShapeDtypeStruct((ROW * ZL, count // ZL, total // ROW), jnp.float32),
        in_specs=[FULL, FULL],
        out_specs=FULL,
        compiler_params=params(),
        cost_estimate=pl.CostEstimate(
            flops=6 * count * total * total, bytes_accessed=20 * count * total, transcendentals=0
        ),
        name="arrange_rows",
    )(order, value)


def share(value):
    copies = jnp.broadcast_to(value[None], (X,) + value.shape)
    return lax.all_to_all(copies, "x", 0, 0, tiled=False)


def local(snapshots, snapshot_order):
    held, cells = snapshots.shape
    total = held * ROW
    factor = 1.0 / (cells * Y * ZL * X * CORE)
    core = lax.axis_index("core")
    row = lax.axis_index("row")
    place = jnp.stack([row, core, lax.axis_index("x")])
    away = lax.rem(snapshot_order // held - row + ROW, ROW)
    first = jnp.where(core == 0, ROW - 1, 1)
    piece = jnp.where(away == 0, 0, jnp.where(away == 2, 3, jnp.where(away == first, 1, 2)))
    index = piece * held + snapshot_order % held
    mine = index.reshape(Y, ZL, X, CORE, -1)
    mine = lax.dynamic_index_in_dim(mine, lax.axis_index("x"), 2, keepdims=False)
    mine = mine.transpose(2, 0, 1, 3)
    wanted = jnp.where(core == 0, mine[::-1], mine).reshape(total // X, 1)
    own, *sent = split(place, snapshots)
    near_a, near_b, opposite = [both_ways(value, "row", by) for value, by in zip(sent, STEPS)]
    group = jnp.concatenate([own, near_a, near_b], axis=0)
    group = [group] + [both_ways(group, "x", by) for by in STEPS]
    arrays = group + [opposite] + [both_ways(opposite, "x", by) for by in STEPS]
    sources = [(None, (0, 1, 2, 3), m * held) for m in range(3)] + [(None, (4, 5, 6, 7), 0)]
    far, near = panels(place, wanted, held, sources, arrays)
    near = near + lax.ppermute(far, "core", [(0, 1), (1, 0)])
    value = lax.all_to_all(near.reshape(Y, -1, total), "y", 0, 0, tiled=False)
    value = arrange(index.reshape(1, total), value)
    value = lax.all_to_all(value, ("row", "zl"), 0, 0, tiled=False)
    return value.sum(0).T * factor


def solution(mesh):
    fine = Mesh(mesh.devices.reshape(Y, ZL, ROW, X, CORE), ("y", "zl", "row", "x", "core"))
    columns = ("y", "zl", "x", "core")
    return jax.shard_map(
        local, mesh=fine, in_specs=(P("row", columns), P()), out_specs=P("row", columns), check_vma=False
    )
```

```python
import functools

import jax
import jax.numpy as jnp
from jax import lax
from jax.experimental import pallas as pl
from jax.experimental.pallas import tpu as pltpu
from jax.sharding import Mesh, PartitionSpec as P

Y, ZL, ROW, X, CORE = 4, 4, 4, 4, 2
VMEM_BYTES = 40 * 1024 * 1024
FULL = pl.BlockSpec(memory_space=pltpu.VMEM)
SCALARS = pl.BlockSpec(memory_space=pltpu.SMEM)


def params():
    return pltpu.CompilerParams(vmem_limit_bytes=VMEM_BYTES)


def both_ways(value, axis, by):
    n = lax.axis_size(axis)
    pairs = [(i * CORE + c, (i + (by if c == 0 else -by)) % n * CORE + c) for i in range(n) for c in range(CORE)]
    return lax.ppermute(value, (axis, "core"), pairs)


def split_kernel(place, source, *outs):
    row, core = place[0], place[1]
    width = outs[0].shape[-1]
    for out, step in zip(outs, (0, 1 + 2 * core, 3 + 2 * core, 2)):
        start = lax.rem(row + step, ROW) * width
        part = source[:, pl.ds(pl.multiple_of(start, width), width)]
        out[...] = jnp.broadcast_to(part, out.shape)


STEPS = (1, 3, 2)


def split(place, snapshots):
    held, cells = snapshots.shape
    width = cells // ROW
    return pl.pallas_call(
        split_kernel,
        out_shape=[jax.ShapeDtypeStruct((X, held, width), snapshots.dtype)]
        + [jax.ShapeDtypeStruct((held, width), snapshots.dtype)] * (ROW - 1),
        in_specs=[SCALARS, FULL],
        out_specs=[FULL] * ROW,
        compiler_params=params(),
        name="split_cells",
    )(place, snapshots)


def slots(place):
    x, core = place[2], place[1]
    return [lax.rem(x + back, X) for back in (0, 3 + 2 * core, 1 + 2 * core, 2)]


def rows_of(source, at, count, order, arrays):
    kind, which, start = source
    at += start
    if kind == "by_x":
        return [arrays[which][slot, at : at + count, :] for slot in order]
    if kind == "stack":
        return [arrays[which][s, at : at + count, :] for s in range(X)]
    return [arrays[i][at : at + count, :] for i in which]


BLOCK = 256


def multiply(left, out, sources, held, order, arrays):
    for to, source in enumerate(sources):
        for at in range(0, held, BLOCK):
            right = jnp.concatenate(rows_of(source, at, BLOCK, order, arrays), axis=1)
            out[:, to * held + at : to * held + at + BLOCK] = lax.dot_general(
                left, right, (((1,), (1,)), ((), ())), preferred_element_type=jnp.float32
            )


def far_kernel(sources, held, place, wanted, *refs):
    arrays, (far, chosen) = refs[:-2], refs[-2:]
    order = slots(place)
    values = []
    for at in range(0, wanted.shape[0], BLOCK):
        parts = [None] * X
        for m, source in enumerate(sources):
            number = lax.broadcasted_iota(jnp.int32, (BLOCK, held), 1) + m * held
            pick = jnp.where(wanted[at : at + BLOCK, :] == number, 1.0, 0.0).astype(jnp.bfloat16)
            for s, rows in enumerate(rows_of(source, 0, held, order, arrays)):
                term = jnp.dot(pick, rows, preferred_element_type=jnp.float32)
                parts[s] = term if parts[s] is None else parts[s] + term
        values.append(jnp.concatenate(parts, axis=1).astype(jnp.bfloat16))
    chosen[...] = values[1]
    multiply(values[0], far, [sources[m] for m in (0, 2, 1, 3)], held, order, arrays)


def near_kernel(sources, held, place, chosen, *refs):
    arrays, near = refs[:-1], refs[-1]
    multiply(chosen[...], near, sources, held, slots(place), arrays)


def panels(place, wanted, held, sources, arrays):
    width = arrays[0].shape[-1]
    total, depth, half = held * ROW, width * X, wanted.shape[0] // CORE
    panel = jax.ShapeDtypeStruct((half, total), jnp.float32)
    cost = pl.CostEstimate(
        flops=2 * half * total * depth, bytes_accessed=2 * total * depth + 4 * half * total, transcendentals=0
    )
    far, chosen = pl.pallas_call(
        functools.partial(far_kernel, sources, held),
        out_shape=[panel, jax.ShapeDtypeStruct((half, depth), arrays[0].dtype)],
        in_specs=[SCALARS] + [FULL] * (1 + len(arrays)),
        out_specs=[FULL] * 2,
        compiler_params=params(),
        cost_estimate=cost,
        name="far_panel",
    )(place, wanted, *arrays)
    near = pl.pallas_call(
        functools.partial(near_kernel, sources, held),
        out_shape=panel,
        in_specs=[SCALARS] + [FULL] * (1 + len(arrays)),
        out_specs=FULL,
        compiler_params=params(),
        cost_estimate=cost,
        name="near_panel",
    )(place, chosen, *arrays)
    return far, near


def arrange_kernel(order, value, out):
    whole = (value[0] + value[1]) + (value[2] + value[3])
    high = whole.astype(jnp.bfloat16)
    rest = whole - high.astype(jnp.float32)
    middle = rest.astype(jnp.bfloat16)
    low = (rest - middle.astype(jnp.float32)).astype(jnp.bfloat16)
    parts = jnp.concatenate([high, middle, low], axis=0)
    count, total = whole.shape
    _, unit, held = out.shape
    block = 256
    for at in range(0, total, block):
        number = lax.broadcasted_iota(jnp.int32, (total, block), 0)
        pick = jnp.where(order[:, at : at + block] == number, 1.0, 0.0).astype(jnp.bfloat16)
        moved = jnp.dot(parts, pick, preferred_element_type=jnp.float32)
        moved = (moved[:count] + moved[count : 2 * count]) + moved[2 * count :]
        row, lane = at // held, at % held
        for zl in range(ZL):
            out[row * ZL + zl, :, lane : lane + block] = moved[zl * unit : (zl + 1) * unit]


def arrange(order, value):
    _, count, total = value.shape
    return pl.pallas_call(
        arrange_kernel,
        out_shape=jax.ShapeDtypeStruct((ROW * ZL, count // ZL, total // ROW), jnp.float32),
        in_specs=[FULL, FULL],
        out_specs=FULL,
        compiler_params=params(),
        cost_estimate=pl.CostEstimate(
            flops=6 * count * total * total, bytes_accessed=20 * count * total, transcendentals=0
        ),
        name="arrange_rows",
    )(order, value)


def share(value):
    if value.ndim == 2:
        value = jnp.broadcast_to(value[None], (X,) + value.shape)
    return lax.all_to_all(value, "x", 0, 0, tiled=False)


def local(snapshots, snapshot_order):
    held, cells = snapshots.shape
    total = held * ROW
    factor = 1.0 / (cells * Y * ZL * X * CORE)
    core = lax.axis_index("core")
    row = lax.axis_index("row")
    place = jnp.stack([row, core, lax.axis_index("x")])
    away = lax.rem(snapshot_order // held - row + ROW, ROW)
    first = jnp.where(core == 0, ROW - 1, 1)
    piece = jnp.where(away == 0, 0, jnp.where(away == 2, 3, jnp.where(away == first, 1, 2)))
    index = piece * held + snapshot_order % held
    mine = index.reshape(Y, ZL, X, CORE, -1)
    mine = lax.dynamic_index_in_dim(mine, lax.axis_index("x"), 2, keepdims=False)
    mine = mine.transpose(2, 0, 1, 3)
    wanted = jnp.where(core == 0, mine[::-1], mine).reshape(total // X, 1)
    own, *sent = split(place, snapshots)
    near_a, near_b, opposite = [both_ways(value, "row", by) for value, by in zip(sent, STEPS)]
    arrays = [share(own), share(near_a)]
    for value in (near_b, opposite):
        arrays += [value] + [both_ways(value, "x", by) for by in STEPS]
    sources = [("by_x", 0, 0), ("by_x", 1, 0), (None, (2, 3, 4, 5), 0), (None, (6, 7, 8, 9), 0)]
    far, near = panels(place, wanted, held, sources, arrays)
    near = near + lax.ppermute(far, "core", [(0, 1), (1, 0)])
    value = lax.all_to_all(near.reshape(Y, -1, total), "y", 0, 0, tiled=False)
    value = arrange(index.reshape(1, total), value)
    value = lax.all_to_all(value, ("row", "zl"), 0, 0, tiled=False)
    return value.sum(0).T * factor


def solution(mesh):
    fine = Mesh(mesh.devices.reshape(Y, ZL, ROW, X, CORE), ("y", "zl", "row", "x", "core"))
    columns = ("y", "zl", "x", "core")
    return jax.shard_map(
        local, mesh=fine, in_specs=(P("row", columns), P()), out_specs=P("row", columns), check_vma=False
    )
```

```python
import functools

import jax
import jax.numpy as jnp
from jax import lax
from jax.experimental import pallas as pl
from jax.experimental.pallas import tpu as pltpu
from jax.sharding import Mesh, PartitionSpec as P

Y, ZL, ROW, X, CORE = 4, 4, 4, 4, 2
VMEM_BYTES = 40 * 1024 * 1024
FULL = pl.BlockSpec(memory_space=pltpu.VMEM)
SCALARS = pl.BlockSpec(memory_space=pltpu.SMEM)


def params():
    return pltpu.CompilerParams(vmem_limit_bytes=VMEM_BYTES)


def both_ways(value, axis, by):
    n = lax.axis_size(axis)
    pairs = [(i * CORE + c, (i + (by if c == 0 else -by)) % n * CORE + c) for i in range(n) for c in range(CORE)]
    return lax.ppermute(value, (axis, "core"), pairs)


def split_kernel(place, source, *outs):
    row, core = place[0], place[1]
    width = outs[0].shape[-1]
    for out, step in zip(outs, (0, 1 + 2 * core, 3 + 2 * core, 2)):
        start = lax.rem(row + step, ROW) * width
        part = source[:, pl.ds(pl.multiple_of(start, width), width)]
        out[...] = jnp.broadcast_to(part, out.shape)


STEPS = (1, 3, 2)


def split(place, snapshots):
    held, cells = snapshots.shape
    width = cells // ROW
    return pl.pallas_call(
        split_kernel,
        out_shape=[jax.ShapeDtypeStruct((X, held, width), snapshots.dtype)]
        + [jax.ShapeDtypeStruct((held, width), snapshots.dtype)] * (ROW - 1),
        in_specs=[SCALARS, FULL],
        out_specs=[FULL] * ROW,
        compiler_params=params(),
        name="split_cells",
    )(place, snapshots)


def slots(place):
    x, core = place[2], place[1]
    return [lax.rem(x + back, X) for back in (0, 3 + 2 * core, 1 + 2 * core, 2)]


def rows_of(source, at, count, order, arrays):
    kind, which, start = source
    at += start
    if kind == "by_x":
        return [arrays[which][slot, at : at + count, :] for slot in order]
    if kind == "stack":
        return [arrays[which][s, at : at + count, :] for s in range(X)]
    return [arrays[i][at : at + count, :] for i in which]


BLOCK = 256


def multiply(left, out, sources, held, order, arrays):
    for to, source in enumerate(sources):
        for at in range(0, held, BLOCK):
            right = jnp.concatenate(rows_of(source, at, BLOCK, order, arrays), axis=1)
            out[:, to * held + at : to * held + at + BLOCK] = lax.dot_general(
                left, right, (((1,), (1,)), ((), ())), preferred_element_type=jnp.float32
            )


def far_kernel(sources, held, place, far_wanted, near_wanted, *refs):
    arrays, (far, chosen) = refs[:-2], refs[-2:]
    order = slots(place)
    values = []
    for wanted in (far_wanted, near_wanted):
        parts = [None] * X
        for m, source in enumerate(sources):
            number = lax.broadcasted_iota(jnp.int32, (wanted.shape[0], held), 1) + m * held
            pick = jnp.where(wanted[...] == number, 1.0, 0.0).astype(jnp.bfloat16)
            for s, rows in enumerate(rows_of(source, 0, held, order, arrays)):
                term = jnp.dot(pick, rows, preferred_element_type=jnp.float32)
                parts[s] = term if parts[s] is None else parts[s] + term
        values.append(jnp.concatenate(parts, axis=1).astype(jnp.bfloat16))
    chosen[...] = values[1]
    multiply(values[0], far, [sources[m] for m in (0, 2, 1, 3)], held, order, arrays)


def near_kernel(sources, held, place, chosen, *refs):
    arrays, near = refs[:-1], refs[-1]
    multiply(chosen[...], near, sources, held, slots(place), arrays)


def panels(place, wanted, held, sources, arrays):
    width = arrays[0].shape[-1]
    total, depth, half = held * ROW, width * X, wanted[0].shape[0]
    panel = jax.ShapeDtypeStruct((half, total), jnp.float32)
    cost = pl.CostEstimate(
        flops=2 * half * total * depth, bytes_accessed=2 * total * depth + 4 * half * total, transcendentals=0
    )
    far, chosen = pl.pallas_call(
        functools.partial(far_kernel, sources, held),
        out_shape=[panel, jax.ShapeDtypeStruct((half, depth), arrays[0].dtype)],
        in_specs=[SCALARS] + [FULL] * (2 + len(arrays)),
        out_specs=[FULL] * 2,
        compiler_params=params(),
        cost_estimate=cost,
        name="far_panel",
    )(place, *wanted, *arrays)
    near = pl.pallas_call(
        functools.partial(near_kernel, sources, held),
        out_shape=panel,
        in_specs=[SCALARS] + [FULL] * (1 + len(arrays)),
        out_specs=FULL,
        compiler_params=params(),
        cost_estimate=cost,
        name="near_panel",
    )(place, chosen, *arrays)
    return far, near


def arrange_kernel(order, value, out):
    whole = (value[0] + value[1]) + (value[2] + value[3])
    high = whole.astype(jnp.bfloat16)
    rest = whole - high.astype(jnp.float32)
    middle = rest.astype(jnp.bfloat16)
    low = (rest - middle.astype(jnp.float32)).astype(jnp.bfloat16)
    parts = jnp.concatenate([high, middle, low], axis=0)
    count, total = whole.shape
    _, unit, held = out.shape
    block = 256
    for at in range(0, total, block):
        number = lax.broadcasted_iota(jnp.int32, (total, block), 0)
        pick = jnp.where(order[:, at : at + block] == number, 1.0, 0.0).astype(jnp.bfloat16)
        moved = jnp.dot(parts, pick, preferred_element_type=jnp.float32)
        moved = (moved[:count] + moved[count : 2 * count]) + moved[2 * count :]
        row, lane = at // held, at % held
        for zl in range(ZL):
            out[row * ZL + zl, :, lane : lane + block] = moved[zl * unit : (zl + 1) * unit]


def arrange(order, value):
    _, count, total = value.shape
    return pl.pallas_call(
        arrange_kernel,
        out_shape=jax.ShapeDtypeStruct((ROW * ZL, count // ZL, total // ROW), jnp.float32),
        in_specs=[FULL, FULL],
        out_specs=FULL,
        compiler_params=params(),
        cost_estimate=pl.CostEstimate(
            flops=6 * count * total * total, bytes_accessed=20 * count * total, transcendentals=0
        ),
        name="arrange_rows",
    )(order, value)


def share(value):
    if value.ndim == 2:
        value = jnp.broadcast_to(value[None], (X,) + value.shape)
    return lax.all_to_all(value, "x", 0, 0, tiled=False)


def local(snapshots, snapshot_order):
    held, cells = snapshots.shape
    total = held * ROW
    factor = 1.0 / (cells * Y * ZL * X * CORE)
    core = lax.axis_index("core")
    row = lax.axis_index("row")
    place = jnp.stack([row, core, lax.axis_index("x")])
    away = lax.rem(snapshot_order // held - row + ROW, ROW)
    first = jnp.where(core == 0, ROW - 1, 1)
    piece = jnp.where(away == 0, 0, jnp.where(away == 2, 3, jnp.where(away == first, 1, 2)))
    index = piece * held + snapshot_order % held
    mine = index.reshape(Y, ZL, X, CORE, -1)
    mine = lax.dynamic_index_in_dim(mine, lax.axis_index("x"), 2, keepdims=False)
    mine = mine.transpose(2, 0, 1, 3)
    wanted = [
        jnp.where(core == 0, mine[1], mine[0]).reshape(-1, 1),
        jnp.where(core == 0, mine[0], mine[1]).reshape(-1, 1),
    ]
    own, *sent = split(place, snapshots)
    near_a, near_b = [both_ways(value, "row", by) for value, by in zip(sent[:2], STEPS)]
    far_sent, near_b = lax.optimization_barrier((sent[2], near_b))
    opposite = both_ways(far_sent, "row", 2)
    arrays = [share(own)]
    for value in (near_a, near_b, opposite):
        arrays += [value] + [both_ways(value, "x", by) for by in STEPS]
    sources = [("by_x", 0, 0)] + [(None, tuple(range(1 + X * m, 1 + X * m + X)), 0) for m in range(3)]
    far, near = panels(place, wanted, held, sources, arrays)
    near = near + lax.ppermute(far, "core", [(0, 1), (1, 0)])
    value = lax.all_to_all(near.reshape(Y, -1, total), "y", 0, 0, tiled=False)
    value = arrange(index.reshape(1, total), value)
    value = lax.all_to_all(value, ("row", "zl"), 0, 0, tiled=False)
    return value.sum(0).T * factor


def solution(mesh):
    fine = Mesh(mesh.devices.reshape(Y, ZL, ROW, X, CORE), ("y", "zl", "row", "x", "core"))
    columns = ("y", "zl", "x", "core")
    return jax.shard_map(
        local, mesh=fine, in_specs=(P("row", columns), P()), out_specs=P("row", columns), check_vma=False
    )
```

```python
import functools

import jax
import jax.numpy as jnp
from jax import lax
from jax.experimental import pallas as pl
from jax.experimental.pallas import tpu as pltpu
from jax.sharding import Mesh, PartitionSpec as P

Y, ZL, ROW, X, CORE = 4, 4, 4, 4, 2
VMEM_BYTES = 40 * 1024 * 1024
FULL = pl.BlockSpec(memory_space=pltpu.VMEM)
SCALARS = pl.BlockSpec(memory_space=pltpu.SMEM)


def params():
    return pltpu.CompilerParams(vmem_limit_bytes=VMEM_BYTES)


def both_ways(value, axis, by):
    n = lax.axis_size(axis)
    pairs = [(i * CORE + c, (i + (by if c == 0 else -by)) % n * CORE + c) for i in range(n) for c in range(CORE)]
    return lax.ppermute(value, (axis, "core"), pairs)


def split_kernel(place, source, *outs):
    row, core = place[0], place[1]
    width = outs[0].shape[-1]
    for out, step in zip(outs, (0, 1 + 2 * core, 3 + 2 * core, 2)):
        start = lax.rem(row + step, ROW) * width
        part = source[:, pl.ds(pl.multiple_of(start, width), width)]
        out[...] = jnp.broadcast_to(part, out.shape)


STEPS = (1, 3, 2)


def split(place, snapshots):
    held, cells = snapshots.shape
    width = cells // ROW
    return pl.pallas_call(
        split_kernel,
        out_shape=[jax.ShapeDtypeStruct((X, held, width), snapshots.dtype)]
        + [jax.ShapeDtypeStruct((held, width), snapshots.dtype)] * (ROW - 1),
        in_specs=[SCALARS, FULL],
        out_specs=[FULL] * ROW,
        compiler_params=params(),
        name="split_cells",
    )(place, snapshots)


def slots(place):
    x, core = place[2], place[1]
    return [lax.rem(x + back, X) for back in (0, 3 + 2 * core, 1 + 2 * core, 2)]


def rows_of(source, at, count, order, arrays):
    kind, which, start = source
    at += start
    if kind == "by_x":
        return [arrays[which][slot, at : at + count, :] for slot in order]
    if kind == "stack":
        return [arrays[which][s, at : at + count, :] for s in range(X)]
    return [arrays[i][at : at + count, :] for i in which]


BLOCK = 256


def multiply(left, out, sources, held, order, arrays):
    for to, source in enumerate(sources):
        for at in range(0, held, BLOCK):
            right = jnp.concatenate(rows_of(source, at, BLOCK, order, arrays), axis=1)
            out[:, to * held + at : to * held + at + BLOCK] = lax.dot_general(
                left, right, (((1,), (1,)), ((), ())), preferred_element_type=jnp.float32
            )


def pick_columns(wanted, sources, held, order, arrays):
    parts = [None] * X
    for m, source in enumerate(sources):
        number = lax.broadcasted_iota(jnp.int32, (wanted.shape[0], held), 1) + m * held
        pick = jnp.where(wanted[...] == number, 1.0, 0.0).astype(jnp.bfloat16)
        for s, rows in enumerate(rows_of(source, 0, held, order, arrays)):
            term = jnp.dot(pick, rows, preferred_element_type=jnp.float32)
            parts[s] = term if parts[s] is None else parts[s] + term
    return jnp.concatenate(parts, axis=1).astype(jnp.bfloat16)


def panel_kernel(sources, lanes_of, held, place, wanted, *refs):
    arrays, out = refs[:-1], refs[-1]
    order = slots(place)
    chosen = pick_columns(wanted, sources, held, order, arrays)
    multiply(chosen, out, [sources[m] for m in lanes_of], held, order, arrays)


def panels(place, wanted, held, sources, arrays):
    width = arrays[0].shape[-1]
    total, depth, half = held * ROW, width * X, wanted[0].shape[0]
    panel = jax.ShapeDtypeStruct((half, total), jnp.float32)
    cost = pl.CostEstimate(
        flops=2 * half * total * depth, bytes_accessed=2 * total * depth + 4 * half * total, transcendentals=0
    )
    def call(columns, lanes_of, name):
        return pl.pallas_call(
            functools.partial(panel_kernel, sources, lanes_of, held),
            out_shape=panel,
            in_specs=[SCALARS] + [FULL] * (1 + len(arrays)),
            out_specs=FULL,
            compiler_params=params(),
            cost_estimate=cost,
            name=name,
        )(place, columns, *arrays)

    return call(wanted[0], (0, 2, 1, 3), "far_panel"), call(wanted[1], (0, 1, 2, 3), "near_panel")


def arrange_kernel(order, value, out):
    whole = (value[0] + value[1]) + (value[2] + value[3])
    high = whole.astype(jnp.bfloat16)
    rest = whole - high.astype(jnp.float32)
    middle = rest.astype(jnp.bfloat16)
    low = (rest - middle.astype(jnp.float32)).astype(jnp.bfloat16)
    parts = jnp.concatenate([high, middle, low], axis=0)
    count, total = whole.shape
    _, unit, held = out.shape
    block = 256
    for at in range(0, total, block):
        number = lax.broadcasted_iota(jnp.int32, (total, block), 0)
        pick = jnp.where(order[:, at : at + block] == number, 1.0, 0.0).astype(jnp.bfloat16)
        moved = jnp.dot(parts, pick, preferred_element_type=jnp.float32)
        moved = (moved[:count] + moved[count : 2 * count]) + moved[2 * count :]
        row, lane = at // held, at % held
        for zl in range(ZL):
            out[row * ZL + zl, :, lane : lane + block] = moved[zl * unit : (zl + 1) * unit]


def arrange(order, value):
    _, count, total = value.shape
    return pl.pallas_call(
        arrange_kernel,
        out_shape=jax.ShapeDtypeStruct((ROW * ZL, count // ZL, total // ROW), jnp.float32),
        in_specs=[FULL, FULL],
        out_specs=FULL,
        compiler_params=params(),
        cost_estimate=pl.CostEstimate(
            flops=6 * count * total * total, bytes_accessed=20 * count * total, transcendentals=0
        ),
        name="arrange_rows",
    )(order, value)


def share(value):
    if value.ndim == 2:
        value = jnp.broadcast_to(value[None], (X,) + value.shape)
    return lax.all_to_all(value, "x", 0, 0, tiled=False)


def local(snapshots, snapshot_order):
    held, cells = snapshots.shape
    total = held * ROW
    factor = 1.0 / (cells * Y * ZL * X * CORE)
    core = lax.axis_index("core")
    row = lax.axis_index("row")
    place = jnp.stack([row, core, lax.axis_index("x")])
    away = lax.rem(snapshot_order // held - row + ROW, ROW)
    first = jnp.where(core == 0, ROW - 1, 1)
    piece = jnp.where(away == 0, 0, jnp.where(away == 2, 3, jnp.where(away == first, 1, 2)))
    index = piece * held + snapshot_order % held
    mine = index.reshape(Y, ZL, X, CORE, -1)
    mine = lax.dynamic_index_in_dim(mine, lax.axis_index("x"), 2, keepdims=False)
    mine = mine.transpose(2, 0, 1, 3)
    wanted = [
        jnp.where(core == 0, mine[1], mine[0]).reshape(-1, 1),
        jnp.where(core == 0, mine[0], mine[1]).reshape(-1, 1),
    ]
    own, *sent = split(place, snapshots)
    near_a, near_b = [both_ways(value, "row", by) for value, by in zip(sent[:2], STEPS)]
    far_sent, near_b = lax.optimization_barrier((sent[2], near_b))
    opposite = both_ways(far_sent, "row", 2)
    arrays = [share(own)]
    for value in (near_a, near_b, opposite):
        arrays += [value] + [both_ways(value, "x", by) for by in STEPS]
    sources = [("by_x", 0, 0)] + [(None, tuple(range(1 + X * m, 1 + X * m + X)), 0) for m in range(3)]
    far, near = panels(place, wanted, held, sources, arrays)
    near = near + lax.ppermute(far, "core", [(0, 1), (1, 0)])
    value = lax.all_to_all(near.reshape(Y, -1, total), "y", 0, 0, tiled=False)
    value = arrange(index.reshape(1, total), value)
    value = lax.all_to_all(value, ("row", "zl"), 0, 0, tiled=False)
    return value.sum(0).T * factor


def solution(mesh):
    fine = Mesh(mesh.devices.reshape(Y, ZL, ROW, X, CORE), ("y", "zl", "row", "x", "core"))
    columns = ("y", "zl", "x", "core")
    return jax.shard_map(
        local, mesh=fine, in_specs=(P("row", columns), P()), out_specs=P("row", columns), check_vma=False
    )
```
